128 devices in a mesh: row: 16 (over x, z), col: 8 (over y, core).
Axes of the slice: x: 4, y: 4, z: 4, core: 2. Of those that a mesh axis runs over, the one named last changes fastest.
Arguments:
- ancestor_inv: float32 [6144, 6144], P('row', 'col'), as said below
- panel_one: float32 [6144, 2048], P('col', 'row'), may hold values from -0.078125 to 0.078125
- panel_two: float32 [6144, 4096], P('col', 'row'), may hold values from -0.078125 to 0.078125
- parent_block: float32 [16, 256, 256], P('col'), may hold values from -0.375 to 0.375
- diag_one: float32 [8, 256, 256], P('col'), may hold values from -6 to 6
- diag_two: float32 [16, 256, 256], P('col'), may hold values from -6 to 6
- pattern_one: int32 [24, 8], replicated, may hold values 0 or 1
- pattern_two: int32 [24, 16], replicated, may hold values 0 or 1
Outputs:
- inv_one: float32 [6144, 2048], P('row', 'col')
- diag_inv_one: float32 [8, 256, 256], P('col')
- inv_two: float32 [6144, 4096], P('row', 'col')
- inv_par: float32 [16, 256, 256], P('col')
- diag_inv_two: float32 [16, 256, 256], P('col')
The draws below stay inside these ranges and needn't reach their ends.
Inputs may be any that keep to these rules, and one draw needn't show every extreme that they name: `ancestor_inv`: equal to its own transpose.
All inputs are finite; a program needn't handle non-finite values.
Results may differ from the reference program's by a relative error of at most 0.000071.
Values sent between devices are 32-bit elements; how exact they have to be, the bound alone decides.
No kernel may reach another device: no remote copies, remote signals or barrier semaphores. Data moves between devices by JAX's collectives and lax.ppermute only.
A program may use at most 128 MiB of HBM per device.

```python
import math
import jax
import jax.numpy as jnp
from jax import lax

BLOCK = 256
ANC_BLK = 24
CHILDREN = 2
ORDER = 6144
PARENTS = 8
KIDS = 16


def draw_ancestor_inv(key, part):
    key = jax.random.fold_in(key, 7)
    key_noise, key_level = jax.random.split(key)
    mat_order = ANC_BLK * BLOCK
    rough_part = jnp.clip(jax.random.normal(key_noise, (mat_order, mat_order), jnp.float32), -5.0, 5.0)
    diag_level = jnp.exp(jax.random.uniform(key_level, (mat_order,), jnp.float32, math.log(0.02), math.log(0.2)))
    symmetric = (rough_part + rough_part.T) * 0.7071
    positions = jnp.arange(mat_order)
    on_diagonal = positions[:, None] == positions[None, :]
    return symmetric + jnp.where(on_diagonal, math.sqrt(mat_order) * diag_level[None, :], 0.0)


def place_ends(drawn, rng, low, high):
    longest = drawn.shape.index(max(drawn.shape))
    spots = []
    for shift in (0, 1):
        where = [jax.random.randint(jax.random.fold_in(rng, axis), (), 0, length) for axis, length in enumerate(drawn.shape)]
        where[longest] = (where[longest] + shift) % drawn.shape[longest]
        spots.append(tuple(where))
    return drawn.at[spots[0]].set(low).at[spots[1]].set(high)


def level_of(key, extent, shards, low, largest):
    gain = 1.0
    for dim, blocks in shards:
        draws = jax.random.uniform(jax.random.fold_in(jax.random.fold_in(key, 6), dim), (blocks,), jnp.float32, low / len(shards), largest / len(shards))
        gain = gain * jnp.repeat(jnp.exp(draws), extent[dim] // blocks).reshape((-1,) + (1,) * (len(extent) - 1 - dim))
    return gain


def normal_values(stream_key, shape, scale, reach, cuts=(), kind=jnp.bfloat16):
    factor_of = level_of(stream_key, shape, cuts, -0.22, 0.18) if cuts else 1.0
    array = jax.random.normal(stream_key, shape, jnp.float32) * scale * factor_of
    return jnp.minimum(jnp.maximum(array, -reach), reach).astype(kind)


def setup_inputs(seed: int = 0) -> dict:
    seeds = jax.random.split(jax.random.key(seed), 9)
    return {
        "ancestor_inv": draw_ancestor_inv(jax.random.fold_in(seeds[8], 71), 0),
        "panel_one": normal_values(seeds[1], (ORDER, PARENTS * BLOCK), ORDER ** -0.5, 0.078125, ((0, 8), (1, 16)), jnp.float32),
        "panel_two": normal_values(seeds[2], (ORDER, KIDS * BLOCK), ORDER ** -0.5, 0.078125, ((0, 8), (1, 16)), jnp.float32),
        "parent_block": normal_values(seeds[3], (KIDS, BLOCK, BLOCK), BLOCK ** -0.5, 0.375, ((0, 8),), jnp.float32),
        "diag_one": normal_values(seeds[4], (PARENTS, BLOCK, BLOCK), 1.0, 6.0, ((0, 8),), jnp.float32),
        "diag_two": normal_values(seeds[5], (KIDS, BLOCK, BLOCK), 1.0, 6.0, ((0, 8),), jnp.float32),
        "pattern_one": place_ends((jax.random.randint(seeds[6], (ANC_BLK, PARENTS), 0, 4) < 3).astype(jnp.int32), jax.random.fold_in(seeds[6], 1), 0, 1),
        "pattern_two": place_ends((jax.random.randint(seeds[7], (ANC_BLK, KIDS), 0, 4) < 3).astype(jnp.int32), jax.random.fold_in(seeds[7], 1), 0, 1),
    }


HIGHEST = lax.Precision.HIGHEST


def expand_pattern(pattern):
    return jnp.repeat(jnp.repeat(pattern.astype(jnp.float32), BLOCK, axis=0), BLOCK, axis=1)


def reference(ancestor_inv, panel_one, panel_two, parent_block, diag_one, diag_two, pattern_one, pattern_two):
    order_rows = ancestor_inv.shape[0]
    child_pattern = pattern_two * jnp.repeat(pattern_one, CHILDREN, axis=1)
    lone = panel_one * expand_pattern(pattern_one)
    ltwo = panel_two * expand_pattern(child_pattern)
    inv_one = -jnp.dot(ancestor_inv, lone, precision=HIGHEST)
    lone_b = lone.reshape(order_rows, -1, BLOCK)
    inv_one_b = inv_one.reshape(order_rows, -1, BLOCK)
    diag_inv_one = diag_one - jnp.einsum("mpa,mpb->pab", lone_b, inv_one_b, precision=HIGHEST)
    inherited = jnp.repeat(inv_one_b, CHILDREN, axis=1)
    cross = jnp.einsum("mpa,pab->mpb", inherited, parent_block, precision=HIGHEST)
    inv_two = -(jnp.dot(ancestor_inv, ltwo, precision=HIGHEST) + cross.reshape(order_rows, -1))
    ltwo_b = ltwo.reshape(order_rows, -1, BLOCK)
    inv_two_b = inv_two.reshape(order_rows, -1, BLOCK)
    parent_diag = jnp.repeat(diag_inv_one, CHILDREN, axis=0)
    inv_par = -(jnp.einsum("mpa,mpb->pab", inherited, ltwo_b, precision=HIGHEST)
                + jnp.einsum("pab,pbc->pac", parent_diag, parent_block, precision=HIGHEST))
    diag_inv_two = (diag_two - jnp.einsum("mpa,mpb->pab", ltwo_b, inv_two_b, precision=HIGHEST)
                    - jnp.einsum("pba,pbc->pac", parent_block, inv_par, precision=HIGHEST))
    return inv_one, diag_inv_one, inv_two, inv_par, diag_inv_two
```

```python
import jax
import jax.numpy as jnp
from jax import lax
from jax.sharding import Mesh, PartitionSpec as P

BLOCK = 256
CHILDREN = 2
HIGH = lax.Precision.HIGH
HIGHEST = lax.Precision.HIGHEST


def ring(axis, shift):
    size = lax.axis_size(axis)
    return [(i, (i + shift) % size) for i in range(size)]


def fetch(value, axis, shift):
    return lax.ppermute(value, axis, ring(axis, -shift))


def swap(value):
    return lax.ppermute(value, "core", [(0, 1), (1, 0)])


def pick(stack, index):
    return lax.dynamic_index_in_dim(stack, index, axis=0, keepdims=False)


def gather_ring(value, axis):
    half = value.shape[0] // 2
    after = fetch(value, axis, 1)
    before = fetch(value, axis, -1)
    far_low = fetch(after[:half], axis, 1)
    far_high = fetch(before[half:], axis, -1)
    return [value, after, before, jnp.concatenate((far_low, far_high), axis=0)]


def block_mask(pattern, row_first, row_count, col_first, col_count):
    widened = jnp.repeat(pattern.astype(jnp.float32), BLOCK, axis=1)
    picked = lax.dynamic_slice(
        widened, (row_first // BLOCK, col_first), (row_count // BLOCK, col_count)
    )
    return jnp.repeat(picked, BLOCK, axis=0)


OFFSETS = (0, 1, -1, 2)
SLOT = {0: 0, 1: 1, -1: 2, 2: 3}


def slot_of(offset):
    offset = offset % 4
    return jnp.where(offset == 2, 3, jnp.where(offset == 3, 2, offset))


def local(
    ancestor_inv, panel_one, panel_two, parent_block, diag_one, diag_two, pattern_one, pattern_two
):
    x, z, y, core = (lax.axis_index(a) for a in ("x", "z", "y", "core"))
    row_index = x * 4 + z
    col_index = y * 2 + core
    panel_rows, w1 = panel_one.shape
    w2 = panel_two.shape[1]
    span = w1 + w2
    strip = ancestor_inv.shape[0]
    half = strip // 2
    child_pattern = pattern_two * jnp.repeat(pattern_one, CHILDREN, axis=1)
    with jax.named_scope("mask"):
        lhs = jnp.concatenate(
            (
                panel_one
                * block_mask(pattern_one, col_index * panel_rows, panel_rows, row_index * w1, w1),
                panel_two
                * block_mask(child_pattern, col_index * panel_rows, panel_rows, row_index * w2, w2),
            ),
            axis=1,
        )
    with jax.named_scope("gather_l"):
        strips = gather_ring(lhs, "x")
        strips = jnp.stack([jnp.concatenate((s, swap(s)), axis=0) for s in strips])
    with jax.named_scope("gather_a"):
        halves = ancestor_inv.reshape(2, half, panel_rows)
        mine = jnp.concatenate((pick(halves, core), swap(pick(halves, 1 - core))), axis=1)
        rows = jnp.concatenate(gather_ring(mine, "z"), axis=0)
    with jax.named_scope("turn_l"):
        parts = lhs.reshape(2, 2, half, span)
        kept = lax.dynamic_index_in_dim(parts, core, axis=1, keepdims=False)
        came = swap(lax.dynamic_index_in_dim(parts, 1 - core, axis=1, keepdims=False))
        four = jnp.concatenate((kept, came), axis=0)
        order = []
        for offset in OFFSETS:
            where = (z + offset) % 4
            order.append(pick(four, jnp.where(where // 2 == core, 0, 2) + where % 2))
        turned = jnp.concatenate(order, axis=0)
        along = gather_ring(turned, "y")
        moved = jnp.where(x == y, along[0], 0.0)
        for offset in (1, -1, 2):
            pairs = [(i * 4 + i, ((i + offset) % 4) * 4 + i) for i in range(4)]
            got = lax.ppermute(along[SLOT[offset]], ("x", "y"), pairs)
            moved = jnp.where((x - y) % 4 == offset % 4, got, moved)
        turned = moved
        one = turned[:, :w1].reshape(4, half, w1)
        even = jnp.concatenate((one[1], one[3], one[0], one[2]), axis=0)
        odd = jnp.concatenate((one[2], one[0], one[3], one[1]), axis=0)
        pairs = [(0, 1), (1, 0), (2, 3), (3, 2)]
        mate = lax.ppermute(jnp.where(z % 2 == 0, even, odd), "z", pairs)
        own = turned[:, :w1]
        full_one = jnp.concatenate(
            (jnp.where(z % 2 == 0, own, mate), jnp.where(z % 2 == 0, mate, own)), axis=1
        )

    def partial(offset):
        return jnp.dot(rows, pick(strips, slot_of(y + offset - x)), precision=HIGH)

    with jax.named_scope("product"):
        far = partial(2)
        mid = far.shape[0] // 2
        low = fetch(far[:mid], "y", -1)
        high = fetch(far[mid:], "y", 1)
        up = partial(1)
        up = jnp.concatenate((up[:mid] + low, up[mid:]), axis=0)
        from_before = fetch(up, "y", -1)
        down = partial(-1)
        down = jnp.concatenate((down[:mid], down[mid:] + high), axis=0)
        from_after = fetch(down, "y", 1)
        total = partial(0) + from_before + from_after
    with jax.named_scope("quad"):
        quad_one = lax.dot_general(
            full_one, total, (((0,), (0,)), ((), ())), precision=HIGH
        )
        quad_two = lax.dot_general(
            turned[:, w1:], total[:, w1:], (((0,), (0,)), ((), ())), precision=HIGH
        )
        quad = jnp.concatenate((quad_one, quad_two), axis=1)
        wide = quad.shape[1]
        quad = quad.reshape(2, BLOCK // 2, wide)
        quad = pick(quad, core) + swap(pick(quad, 1 - core))
        quad = quad.reshape(4, BLOCK // 8, wide)
        acc = pick(quad, x)
        for offset in (1, -1, 2):
            acc = acc + fetch(pick(quad, (x - offset) % 4), "x", offset)
        around = jnp.stack([acc] + [fetch(acc, "x", o) for o in (1, -1, 2)])
        around = jnp.concatenate([pick(around, slot_of(i - x)) for i in range(4)], axis=0)
        around = jnp.stack([around] + [fetch(around, "z", o) for o in (1, -1, 2)])
        keep = [pick(around, slot_of(2 * core + i - z)) for i in range(2)]
        give = jnp.stack([pick(around, slot_of(2 * (1 - core) + i - z)) for i in range(2)])
        came = swap(give)
        sums = [
            jnp.concatenate(
                (jnp.where(core == 0, keep[i], came[i]), jnp.where(core == 0, came[i], keep[i])),
                axis=0,
            )
            for i in range(2)
        ]
    with jax.named_scope("out"):
        blocks = total.reshape(4, half, span)
        parts = jnp.stack(
            [blocks[0]] + [fetch(blocks[SLOT[-o]], "z", o) for o in (1, -1)] + [fetch(blocks[3], "z", 2)]
        )
        keep = jnp.stack([pick(parts, slot_of(2 * core + i - z)) for i in range(2)])
        give = jnp.stack([pick(parts, slot_of(2 * (1 - core) + i - z)) for i in range(2)])
        came = swap(give)
        joined = jnp.concatenate(
            (jnp.where(core == 0, keep, came), jnp.where(core == 0, came, keep)), axis=1
        )
        prod_one = jnp.concatenate((joined[0, :, :w1], joined[1, :, :w1]), axis=1)
        inv_one = -prod_one
        inv_two = jnp.concatenate(
            [
                jnp.dot(prod_one, parent_block[i], precision=HIGH) - joined[i, :, w1:]
                for i in range(2)
            ],
            axis=1,
        )
    with jax.named_scope("diag"):
        first = jnp.concatenate((sums[0][:, :w1], sums[1][:, :w1]), axis=1)
        across = jnp.stack([s[:, w1 : w1 + w2] for s in sums])
        reach = jnp.stack([s[:, w1 + w2 :] for s in sums])
        diag_inv_one = diag_one + first[None]
        inv_par = across - jnp.einsum("ab,pbc->pac", diag_inv_one[0], parent_block, precision=HIGH)
        diag_inv_two = (
            diag_two
            + reach
            - jnp.einsum("pba,pbc->pac", across, parent_block, precision=HIGH)
            - jnp.einsum("pba,pbc->pac", parent_block, inv_par, precision=HIGH)
        )
    return (inv_one, diag_inv_one, inv_two, inv_par, diag_inv_two)


def solution(mesh):
    grid = Mesh(mesh.devices.reshape(4, 4, 4, 2), ("x", "z", "y", "core"))
    row, col = ("x", "z"), ("y", "core")
    return jax.shard_map(
        local,
        mesh=grid,
        in_specs=(
            P(row, col),
            P(col, row),
            P(col, row),
            P(col, None, None),
            P(col, None, None),
            P(col, None, None),
            P(),
            P(),
        ),
        out_specs=(
            P(row, col),
            P(col, None, None),
            P(row, col),
            P(col, None, None),
            P(col, None, None),
        ),
        check_vma=False,
    )
```

```python
import functools

import jax
import jax.numpy as jnp
from jax import lax
from jax.experimental import pallas as pl
from jax.experimental.pallas import tpu as pltpu
from jax.sharding import Mesh, PartitionSpec as P

BLOCK = 256
CHILDREN = 2
HIGH = lax.Precision.HIGH
HIGHEST = lax.Precision.HIGHEST


def fetch(value, axis, shift):
    size = lax.axis_size(axis)
    return lax.ppermute(value, axis, [((i + shift) % size, i) for i in range(size)])


def swap(value):
    return lax.ppermute(value, "core", [(0, 1), (1, 0)])


def split_pairs(step):
    return [(i * 2 + c, (i + (step, -step)[c]) % 4 * 2 + c) for i in range(4) for c in range(2)]


def send(value, axis, step):
    return lax.ppermute(value, (axis, "core"), split_pairs(step))


def after(value, *deps):
    return lax.optimization_barrier((value, *deps))[0] if deps else value


def pick(stack, index):
    return lax.dynamic_index_in_dim(stack, index, axis=0, keepdims=False)


def split(value):
    high = value.astype(jnp.bfloat16)
    return high, (value - high.astype(jnp.float32)).astype(jnp.bfloat16)


def take(refs, to, sems, chosen=None):
    if chosen is None:
        copies = [
            pltpu.make_async_copy(ref, to.at[k], sems.at[k]) for k, ref in enumerate(refs)
        ]
        for copy in copies:
            copy.start()
        return copies
    for k in range(len(refs) // 2):

        @pl.when(chosen == k)
        def _(k=k):
            for p in range(2):
                pltpu.make_async_copy(refs[2 * k + p], to.at[p], sems.at[p]).start()

    return [pltpu.make_async_copy(refs[p], to.at[p], sems.at[p]) for p in range(2)]


def multiply(out, row_high, row_low, strip, strip_high, strip_low):
    deep, chunk = strip.shape[1], 64
    for p in range(2):

        @pl.loop(0, deep // chunk)
        def _(i, p=p):
            high, low = split(strip[p, pl.ds(i * chunk, chunk), :])
            at = pl.ds(p * deep + i * chunk, chunk)
            strip_high[at, :] = high
            strip_low[at, :] = low

    dot = functools.partial(jnp.dot, preferred_element_type=jnp.float32)
    tall = out.shape[0] // 2

    @pl.loop(0, 2)
    def _(r):
        at = pl.ds(pl.multiple_of(r * tall, tall), tall)
        value = dot(row_high[at, :], strip_low[...]) + dot(row_low[at, :], strip_high[...])
        out[at, :] = value + dot(row_high[at, :], strip_high[...])


def first_kernel(places, *refs):
    rows, strips = refs[:4], refs[4:12]
    out_high, out_low, out = refs[12:15]
    row, row_high, row_low, strip, strip_high, strip_low, row_sems, sems = refs[15:]
    row_copies = take(rows, row, row_sems)
    strip_copies = take(strips, strip, sems, places[4])
    half, deep = rows[0].shape[1:]
    chunk = 64
    for k, copy in enumerate(row_copies):
        copy.wait()
        first = places[k] * half
        for p in range(2):

            @pl.loop(0, half // chunk)
            def _(i, k=k, p=p, first=first):
                high, low = split(row[k, p, pl.ds(i * chunk, chunk), :])
                at = pl.ds(pl.multiple_of(first + i * chunk, chunk), chunk)
                row_high[at, pl.ds(p * deep, deep)] = high
                row_low[at, pl.ds(p * deep, deep)] = low

    outs = [
        pltpu.make_async_copy(row_high, out_high, row_sems.at[0]),
        pltpu.make_async_copy(row_low, out_low, row_sems.at[1]),
    ]
    for copy in outs:
        copy.start()
    for copy in strip_copies:
        copy.wait()
    multiply(out, row_high, row_low, strip, strip_high, strip_low)
    for copy in outs:
        copy.wait()


def next_kernel(places, *refs):
    rows, strips = refs[:2], refs[2:10]
    out, row_high, row_low, strip, strip_high, strip_low, row_sems, sems = refs[10:]
    row_copies = [
        pltpu.make_async_copy(ref, to, row_sems.at[p])
        for p, (ref, to) in enumerate(zip(rows, (row_high, row_low)))
    ]
    strip_copies = take(strips, strip, sems, places[0])
    for copy in row_copies:
        copy.start()
    for copy in strip_copies:
        copy.wait()
    for copy in row_copies:
        copy.wait()
    multiply(out, row_high, row_low, strip, strip_high, strip_low)


def product(places, rows, strips):
    vmem, hbm = (pl.BlockSpec(memory_space=m) for m in (pltpu.VMEM, pltpu.HBM))
    deep, wide = strips[0].shape
    first = len(rows) == 4
    tall = 4 * rows[0].shape[1] if first else rows[0].shape[0]
    parts = jax.ShapeDtypeStruct((tall, 2 * deep), jnp.bfloat16)
    out = jax.ShapeDtypeStruct((tall, wide), jnp.float32)
    scratch = [pltpu.VMEM((tall, 2 * deep), jnp.bfloat16)] * 2
    scratch += [pltpu.VMEM((2, deep, wide), jnp.float32)]
    scratch += [pltpu.VMEM((2 * deep, wide), jnp.bfloat16)] * 2
    if first:
        scratch = [pltpu.VMEM((4, *rows[0].shape), jnp.float32)] + scratch
    results = pl.pallas_call(
        first_kernel if first else next_kernel,
        out_shape=[parts, parts, out] if first else [out],
        in_specs=[pl.BlockSpec(memory_space=pltpu.SMEM)] + [hbm] * (len(rows) + 8),
        out_specs=[hbm, hbm, vmem] if first else [vmem],
        scratch_shapes=scratch
        + [pltpu.SemaphoreType.DMA((4 if first else 2,)), pltpu.SemaphoreType.DMA((2,))],
        compiler_params=pltpu.CompilerParams(vmem_limit_bytes=56 * 2**20),
        cost_estimate=pl.CostEstimate(
            flops=tall, bytes_accessed=tall, transcendentals=0
        ),
        name="first_product" if first else "next_product",
    )(jnp.stack(places).astype(jnp.int32), *rows, *strips)
    return results if first else results[0]


def local(
    ancestor_inv, panel_one, panel_two, parent_block, diag_one, diag_two, pattern_one, pattern_two
):
    x, z, y, core = (lax.axis_index(a) for a in ("x", "z", "y", "core"))
    row_index = x * 4 + z
    col_index = y * 2 + core
    panel_rows, w1 = panel_one.shape
    w2 = panel_two.shape[1]
    span = w1 + w2
    half = ancestor_inv.shape[0] // 2
    child_pattern = pattern_two * jnp.repeat(pattern_one, CHILDREN, axis=1)
    with jax.named_scope("gather"):
        halves = ancestor_inv.reshape(2, half, panel_rows)
        given = pick(halves, 1 - core)
        panel_one, panel_two = after(panel_one, given), after(panel_two, given)
        given = swap(given)
    with jax.named_scope("mask"):
        blocks = panel_rows // BLOCK
        mask_one = lax.dynamic_slice(
            pattern_one, (col_index * blocks, row_index // CHILDREN), (blocks, 1)
        )
        mask_two = mask_one * lax.dynamic_slice(
            pattern_two, (col_index * blocks, row_index), (blocks, 1)
        )
        lhs = jnp.concatenate(
            [
                (p.reshape(blocks, BLOCK, -1) * m.astype(jnp.float32)[:, :, None]).reshape(
                    panel_rows, -1
                )
                for p, m in ((panel_one, mask_one), (panel_two, mask_two))
            ],
            axis=1,
        )
    side = jnp.where(core == 0, -1, 1)

    def place(offset):
        offset = offset % 4
        return jnp.where(
            offset == 0, 0, jnp.where(offset == 2, 3, jnp.where(offset == side % 4, 1, 2))
        )

    with jax.named_scope("gather"):
        rows = jnp.stack((pick(halves, core), given))
        lhs = after(lhs, given)
        lhs_other = swap(lhs)
        mine, other = (
            lax.dynamic_index_in_dim(v.reshape(2, 2, half, span), core, axis=1, keepdims=False)
            for v in (lhs, lhs_other)
        )
        source = jnp.concatenate(
            (jnp.where(core == 0, mine, other), jnp.where(core == 0, other, mine)), axis=0
        ).reshape(panel_rows, span)
        source = after(source, rows)
        a_first, a_second = send(rows, "z", 1), send(rows, "z", -1)
        l_first, l_second = send(lhs, "x", 1), send(lhs, "x", -1)
        t_first = send(source, "y", 1)
        t_second = send(after(source, t_first), "y", -1)
        a_first, a_second, l_first, l_second, t_second = lax.optimization_barrier(
            (a_first, a_second, l_first, l_second, t_second)
        )
        a_far, l_far = send(a_first, "z", 1), send(l_first, "x", 1)
        t_far = send(after(t_first, t_second), "y", 1)
        first_other, second_other = swap(l_second), swap(l_first)
        a_far, l_far, t_far, first_other, second_other = lax.optimization_barrier(
            (a_far, l_far, t_far, first_other, second_other)
        )
        far_other = swap(l_far)

    def spread(values):
        return [
            lax.ppermute(
                value,
                ("z", "core"),
                [
                    ((2 * c + j) * 2 + h, ((2 * j + h) ^ turn_over) * 2 + c)
                    for c in range(2)
                    for j in range(2)
                    for h in range(2)
                ],
            )
            for turn_over, value in enumerate(values)
        ]

    def turn(value, offset, which=0):
        pairs = []
        for i in range(4):
            for c, m in ((0, 1), (1, -1)):
                begin = i + which * m
                end = begin + offset * m
                pairs.append(((begin % 4 * 4 + i) * 2 + c, (end % 4 * 4 + i) * 2 + c))
        return lax.ppermute(value, ("x", "y", "core"), pairs)

    strips = (lhs, lhs_other, l_first, first_other, l_second, second_other, l_far, far_other)
    offsets = (0, side, -side, 2)

    def strip_of(offset):
        return place(y + offset - x)

    with jax.named_scope("product"):
        *parts, far = product(
            [(z + o) % 4 for o in offsets] + [strip_of(2)],
            (rows, a_first, a_second, a_far),
            strips,
        )
        far_came = send(far, "y", 1)
        q_step = turn(after(t_far, l_far), 1)
        q_first = turn(after(t_first, l_far), -1)
        near = product([strip_of(side)], [after(p, far) for p in parts], strips)
        near_came = send(near, "y", -1)
        q_far = turn(after(q_step, near), 1, 1)
        q_second = turn(after(t_second, q_first, near), 1)
        last = product([strip_of(-side)], [after(p, near, far_came) for p in parts], strips)
        last = after(last, near_came) + far_came
        last_came = send(last, "y", 1)
    with jax.named_scope("turned"):
        shift = (x - y) % 4
        turned = jnp.where(
            shift == 0,
            source,
            jnp.where(
                shift == 2, q_far, jnp.where(shift == side % 4, q_first, q_second)
            ),
        )
        own = turned[:, :w1]
        mate = lax.ppermute(own, "z", [(0, 1), (1, 0), (2, 3), (3, 2)])
        full_one = jnp.concatenate(
            (jnp.where(z % 2 == 0, own, mate), jnp.where(z % 2 == 0, mate, own)), axis=1
        )
    with jax.named_scope("total"):
        rest = product([strip_of(0)], [after(p, last, turned) for p in parts], strips)
        rest, near_came, last_came = lax.optimization_barrier((rest, near_came, last_came))
        total = rest + near_came + last_came
    with jax.named_scope("out"):
        pairs_of_rows = total.reshape(2, 2 * half, span)
        kept, came = pick(pairs_of_rows, core), swap(pick(pairs_of_rows, 1 - core))
        kept, came = kept.reshape(2, half, span), came.reshape(2, half, span)
        blocks = jnp.concatenate(
            (jnp.where(core == 0, kept, came), jnp.where(core == 0, came, kept)), axis=1
        )
        pieces = []
        for turn_over in range(2):
            pairs = [
                ((2 * c + j) * 2 + h, (2 * h + (j + turn_over) % 2) * 2 + c)
                for c in range(2)
                for j in range(2)
                for h in range(2)
            ]
            pieces.append(lax.ppermute(pick(blocks, (z + turn_over) % 2), ("z", "core"), pairs))
    with jax.named_scope("quad"):
        quad_one = lax.dot_general(full_one, total, (((0,), (0,)), ((), ())), precision=HIGH)
        quad_two = lax.dot_general(
            turned[:, w1:], total[:, w1:], (((0,), (0,)), ((), ())), precision=HIGH
        )
        quad = jnp.concatenate((quad_one, quad_two), axis=1)
        wide = quad.shape[1]
        quad = quad.reshape(2, BLOCK // 2, wide)
        quad = pick(quad, core) + swap(pick(quad, 1 - core))
        first, second = send(quad, "x", 1), send(quad, "x", -1)
        around = quad + first + second + send(first, "x", 1)
        around = after(around, *pieces)
        came = jnp.stack(spread([around] * 4))
        sums = [
            jnp.concatenate([pick(came, (2 * j + h) ^ z) for h in range(2)], axis=0)
            for j in range(2)
        ]
    with jax.named_scope("out"):
        joined = [jnp.where(z % 2 == j, pieces[0], pieces[1]) for j in range(2)]
        prod_one = jnp.concatenate([v[:, :w1] for v in joined], axis=1)
        inv_one = -prod_one
        inv_two = jnp.concatenate(
            [
                jnp.dot(prod_one, parent_block[i], precision=HIGH) - joined[i][:, w1:]
                for i in range(2)
            ],
            axis=1,
        )
    with jax.named_scope("diag"):
        first = jnp.concatenate((sums[0][:, :w1], sums[1][:, :w1]), axis=1)
        across = jnp.stack([s[:, w1 : w1 + w2] for s in sums])
        reach = jnp.stack([s[:, w1 + w2 :] for s in sums])
        diag_inv_one = diag_one + first[None]
        inv_par = across - jnp.einsum("ab,pbc->pac", diag_inv_one[0], parent_block, precision=HIGH)
        diag_inv_two = (
            diag_two
            + reach
            - jnp.einsum("pba,pbc->pac", across, parent_block, precision=HIGH)
            - jnp.einsum("pba,pbc->pac", parent_block, inv_par, precision=HIGH)
        )
    return (inv_one, diag_inv_one, inv_two, inv_par, diag_inv_two)


def solution(mesh):
    grid = Mesh(mesh.devices.reshape(4, 4, 4, 2), ("x", "z", "y", "core"))
    row, col = ("x", "z"), ("y", "core")
    return jax.shard_map(
        local,
        mesh=grid,
        in_specs=(
            P(row, col),
            P(col, row),
            P(col, row),
            P(col, None, None),
            P(col, None, None),
            P(col, None, None),
            P(),
            P(),
        ),
        out_specs=(
            P(row, col),
            P(col, None, None),
            P(row, col),
            P(col, None, None),
            P(col, None, None),
        ),
        check_vma=False,
    )
```

```python
import functools

import jax
import jax.numpy as jnp
from jax import lax
from jax.experimental import pallas as pl
from jax.experimental.pallas import tpu as pltpu
from jax.sharding import Mesh, PartitionSpec as P

BLOCK = 256
CHILDREN = 2
HIGH = lax.Precision.HIGH
HIGHEST = lax.Precision.HIGHEST


def fetch(value, axis, shift):
    size = lax.axis_size(axis)
    return lax.ppermute(value, axis, [((i + shift) % size, i) for i in range(size)])


def swap(value):
    return lax.ppermute(value, "core", [(0, 1), (1, 0)])


def split_pairs(step):
    return [(i * 2 + c, (i + (step, -step)[c]) % 4 * 2 + c) for i in range(4) for c in range(2)]


def send(value, axis, step):
    return lax.ppermute(value, (axis, "core"), split_pairs(step))


def after(value, *deps):
    return lax.optimization_barrier((value, *deps))[0] if deps else value


def pick(stack, index):
    return lax.dynamic_index_in_dim(stack, index, axis=0, keepdims=False)


def split(value):
    high = value.astype(jnp.bfloat16)
    return high, (value - high.astype(jnp.float32)).astype(jnp.bfloat16)


def take(refs, to, sems, chosen=None):
    if chosen is None:
        copies = [
            pltpu.make_async_copy(ref, to.at[k], sems.at[k]) for k, ref in enumerate(refs)
        ]
        for copy in copies:
            copy.start()
        return copies
    for k in range(len(refs) // 2):

        @pl.when(chosen == k)
        def _(k=k):
            for p in range(2):
                pltpu.make_async_copy(refs[2 * k + p], to.at[p], sems.at[p]).start()

    return [pltpu.make_async_copy(refs[p], to.at[p], sems.at[p]) for p in range(2)]


def split_strip(strip, strip_high, strip_low, copies):
    deep, chunk = strip.shape[1], 64
    for p in range(2):
        copies[p].wait()

        @pl.loop(0, deep // chunk)
        def _(i, p=p):
            high, low = split(strip[p, pl.ds(i * chunk, chunk), :])
            at = pl.ds(p * deep + i * chunk, chunk)
            strip_high[at, :] = high
            strip_low[at, :] = low


def multiply(out, row_high, row_low, strip_high, strip_low):
    dot = functools.partial(jnp.dot, preferred_element_type=jnp.float32)
    tall = out.shape[0] // 2

    @pl.loop(0, 2)
    def _(r):
        at = pl.ds(pl.multiple_of(r * tall, tall), tall)
        value = dot(row_high[at, :], strip_low[...]) + dot(row_low[at, :], strip_high[...])
        out[at, :] = value + dot(row_high[at, :], strip_high[...])


def first_kernel(places, *refs):
    rows, strips = refs[:4], refs[4:12]
    out_high, out_low, out = refs[12:15]
    row, row_high, row_low, strip, strip_high, strip_low, row_sems, sems = refs[15:]
    strip_copies = take(strips, strip, sems, places[4])
    row_copies = take(rows, row, row_sems)
    split_strip(strip, strip_high, strip_low, strip_copies)
    half, deep = rows[0].shape[1:]
    chunk = 64
    for k, copy in enumerate(row_copies):
        copy.wait()
        first = places[k] * half
        for p in range(2):

            @pl.loop(0, half // chunk)
            def _(i, k=k, p=p, first=first):
                high, low = split(row[k, p, pl.ds(i * chunk, chunk), :])
                at = pl.ds(pl.multiple_of(first + i * chunk, chunk), chunk)
                row_high[at, pl.ds(p * deep, deep)] = high
                row_low[at, pl.ds(p * deep, deep)] = low

    outs = [
        pltpu.make_async_copy(row_high, out_high, row_sems.at[0]),
        pltpu.make_async_copy(row_low, out_low, row_sems.at[1]),
    ]
    for copy in outs:
        copy.start()
    multiply(out, row_high, row_low, strip_high, strip_low)
    for copy in outs:
        copy.wait()


def next_kernel(places, *refs):
    rows, strips = refs[:2], refs[2:10]
    out, row_high, row_low, strip, strip_high, strip_low, row_sems, sems = refs[10:]
    row_copies = [
        pltpu.make_async_copy(ref, to, row_sems.at[p])
        for p, (ref, to) in enumerate(zip(rows, (row_high, row_low)))
    ]
    strip_copies = take(strips, strip, sems, places[0])
    for copy in row_copies:
        copy.start()
    split_strip(strip, strip_high, strip_low, strip_copies)
    for copy in row_copies:
        copy.wait()
    multiply(out, row_high, row_low, strip_high, strip_low)


def product(places, rows, strips, counted=False):
    vmem, hbm = (pl.BlockSpec(memory_space=m) for m in (pltpu.VMEM, pltpu.HBM))
    deep, wide = strips[0].shape
    first = len(rows) == 4
    tall = 4 * rows[0].shape[1] if first else rows[0].shape[0]
    parts = jax.ShapeDtypeStruct((tall, 2 * deep), jnp.bfloat16)
    out = jax.ShapeDtypeStruct((tall, wide), jnp.float32)
    scratch = [pltpu.VMEM((tall, 2 * deep), jnp.bfloat16)] * 2
    scratch += [pltpu.VMEM((2, deep, wide), jnp.float32)]
    scratch += [pltpu.VMEM((2 * deep, wide), jnp.bfloat16)] * 2
    if first:
        scratch = [pltpu.VMEM((4, *rows[0].shape), jnp.float32)] + scratch
    results = pl.pallas_call(
        first_kernel if first else next_kernel,
        out_shape=[parts, parts, out] if first else [out],
        in_specs=[pl.BlockSpec(memory_space=pltpu.SMEM)] + [hbm] * (len(rows) + 8),
        out_specs=[hbm, hbm, vmem] if first else [vmem],
        scratch_shapes=scratch
        + [pltpu.SemaphoreType.DMA((4 if first else 2,)), pltpu.SemaphoreType.DMA((2,))],
        compiler_params=pltpu.CompilerParams(vmem_limit_bytes=56 * 2**20),
        cost_estimate=pl.CostEstimate(
            flops=8 * 10**9 if counted else tall, bytes_accessed=tall, transcendentals=0
        ),
        name="first_product" if first else "next_product",
    )(jnp.stack(places).astype(jnp.int32), *rows, *strips)
    return results if first else results[0]


def local(
    ancestor_inv, panel_one, panel_two, parent_block, diag_one, diag_two, pattern_one, pattern_two
):
    x, z, y, core = (lax.axis_index(a) for a in ("x", "z", "y", "core"))
    row_index = x * 4 + z
    col_index = y * 2 + core
    panel_rows, w1 = panel_one.shape
    w2 = panel_two.shape[1]
    span = w1 + w2
    half = ancestor_inv.shape[0] // 2
    child_pattern = pattern_two * jnp.repeat(pattern_one, CHILDREN, axis=1)
    with jax.named_scope("gather"):
        halves = ancestor_inv.reshape(2, half, panel_rows)
        given = pick(halves, 1 - core)
        panel_one, panel_two = after(panel_one, given), after(panel_two, given)
        given = swap(given)
    with jax.named_scope("mask"):
        blocks = panel_rows // BLOCK
        mask_one = lax.dynamic_slice(
            pattern_one, (col_index * blocks, row_index // CHILDREN), (blocks, 1)
        )
        mask_two = mask_one * lax.dynamic_slice(
            pattern_two, (col_index * blocks, row_index), (blocks, 1)
        )
        lhs = jnp.concatenate(
            [
                (p.reshape(blocks, BLOCK, -1) * m.astype(jnp.float32)[:, :, None]).reshape(
                    panel_rows, -1
                )
                for p, m in ((panel_one, mask_one), (panel_two, mask_two))
            ],
            axis=1,
        )
    side = jnp.where(core == 0, -1, 1)

    def place(offset):
        offset = offset % 4
        return jnp.where(
            offset == 0, 0, jnp.where(offset == 2, 3, jnp.where(offset == side % 4, 1, 2))
        )

    with jax.named_scope("gather"):
        rows = jnp.stack((pick(halves, core), given))
        lhs = after(lhs, given)
        lhs_other = swap(lhs)
        mine, other = (
            lax.dynamic_index_in_dim(v.reshape(2, 2, half, span), core, axis=1, keepdims=False)
            for v in (lhs, lhs_other)
        )
        source = jnp.concatenate(
            (jnp.where(core == 0, mine, other), jnp.where(core == 0, other, mine)), axis=0
        ).reshape(panel_rows, span)
        source = after(source, rows)
        a_first, a_second = send(rows, "z", 1), send(rows, "z", -1)
        l_first, l_second = send(lhs, "x", 1), send(lhs, "x", -1)
        t_first = send(source, "y", 1)
        t_second = send(after(source, t_first), "y", -1)
        a_first, a_second, l_first, l_second, t_second = lax.optimization_barrier(
            (a_first, a_second, l_first, l_second, t_second)
        )
        a_far, l_far = send(a_first, "z", 1), send(l_first, "x", 1)
        t_far = send(after(t_first, t_second), "y", 1)
        first_other, second_other = swap(l_second), swap(l_first)
        a_far, l_far, t_far, first_other, second_other = lax.optimization_barrier(
            (a_far, l_far, t_far, first_other, second_other)
        )
        far_other = swap(l_far)

    def spread(values):
        return [
            lax.ppermute(
                value,
                ("z", "core"),
                [
                    ((2 * c + j) * 2 + h, ((2 * j + h) ^ turn_over) * 2 + c)
                    for c in range(2)
                    for j in range(2)
                    for h in range(2)
                ],
            )
            for turn_over, value in enumerate(values)
        ]

    def turn(value, offset, which=0):
        pairs = []
        for i in range(4):
            for c, m in ((0, 1), (1, -1)):
                begin = i + which * m
                end = begin + offset * m
                pairs.append(((begin % 4 * 4 + i) * 2 + c, (end % 4 * 4 + i) * 2 + c))
        return lax.ppermute(value, ("x", "y", "core"), pairs)

    strips = (lhs, lhs_other, l_first, first_other, l_second, second_other, l_far, far_other)
    offsets = (0, side, -side, 2)

    def strip_of(offset):
        return place(y + offset - x)

    with jax.named_scope("product"):
        *parts, far = product(
            [(z + o) % 4 for o in offsets] + [strip_of(2)],
            (rows, a_first, a_second, a_far),
            strips,
        )
        far_came = send(far, "y", 1)
        q_step = turn(after(t_far, l_far), 1)
        q_first = turn(after(t_first, l_far), -1)
        near = product([strip_of(side)], [after(p, far) for p in parts], strips)
        near_came = send(near, "y", -1)
        q_far = turn(after(q_step, near), 1, 1)
        q_second = turn(after(t_second, near), 1)
        last = product([strip_of(-side)], [after(p, near) for p in parts], strips)
        last = last + far_came
        last_came = send(last, "y", 1)
    with jax.named_scope("turned"):
        shift = (x - y) % 4
        turned = jnp.where(
            shift == 0,
            source,
            jnp.where(
                shift == 2, q_far, jnp.where(shift == side % 4, q_first, q_second)
            ),
        )
        own = turned[:, :w1]
        mate = lax.ppermute(own, "z", [(0, 1), (1, 0), (2, 3), (3, 2)])
        full_one = jnp.concatenate(
            (jnp.where(z % 2 == 0, own, mate), jnp.where(z % 2 == 0, mate, own)), axis=1
        )
    with jax.named_scope("total"):
        rest = product([strip_of(0)], [after(p, last, turned, near_came) for p in parts], strips, True)
        rest, near_came, last_came = lax.optimization_barrier((rest, near_came, last_came))
        total = rest + near_came + last_came
    with jax.named_scope("out"):
        pairs_of_rows = total.reshape(2, 2 * half, span)
        kept, came = pick(pairs_of_rows, core), swap(pick(pairs_of_rows, 1 - core))
        kept, came = kept.reshape(2, half, span), came.reshape(2, half, span)
        blocks = jnp.concatenate(
            (jnp.where(core == 0, kept, came), jnp.where(core == 0, came, kept)), axis=1
        )
        pieces = []
        for turn_over in range(2):
            pairs = [
                ((2 * c + j) * 2 + h, (2 * h + (j + turn_over) % 2) * 2 + c)
                for c in range(2)
                for j in range(2)
                for h in range(2)
            ]
            pieces.append(lax.ppermute(pick(blocks, (z + turn_over) % 2), ("z", "core"), pairs))
    with jax.named_scope("quad"):
        quad_one = lax.dot_general(full_one, total, (((0,), (0,)), ((), ())), precision=HIGH)
        quad_two = lax.dot_general(
            turned[:, w1:], total[:, w1:], (((0,), (0,)), ((), ())), precision=HIGH
        )
        quad = jnp.concatenate((quad_one, quad_two), axis=1)
        wide = quad.shape[1]
        quad = quad.reshape(2, BLOCK // 2, wide)
        quad = pick(quad, core) + swap(pick(quad, 1 - core))
        first, second = send(quad, "x", 1), send(quad, "x", -1)
        around = quad + first + second + send(after(first, pieces[1]), "x", 1)
        around = after(around, pieces[0])
        came = jnp.stack(spread([around] * 4))
        sums = [
            jnp.concatenate([pick(came, (2 * j + h) ^ z) for h in range(2)], axis=0)
            for j in range(2)
        ]
    with jax.named_scope("out"):
        joined = [jnp.where(z % 2 == j, pieces[0], pieces[1]) for j in range(2)]
        prod_one = jnp.concatenate([v[:, :w1] for v in joined], axis=1)
        inv_one = -prod_one
        inv_two = jnp.concatenate(
            [
                jnp.dot(prod_one, parent_block[i], precision=HIGH) - joined[i][:, w1:]
                for i in range(2)
            ],
            axis=1,
        )
    with jax.named_scope("diag"):
        first = jnp.concatenate((sums[0][:, :w1], sums[1][:, :w1]), axis=1)
        across = jnp.stack([s[:, w1 : w1 + w2] for s in sums])
        reach = jnp.stack([s[:, w1 + w2 :] for s in sums])
        diag_inv_one = diag_one + first[None]
        inv_par = across - jnp.einsum("ab,pbc->pac", diag_inv_one[0], parent_block, precision=HIGH)
        diag_inv_two = (
            diag_two
            + reach
            - jnp.einsum("pba,pbc->pac", across, parent_block, precision=HIGH)
            - jnp.einsum("pba,pbc->pac", parent_block, inv_par, precision=HIGH)
        )
    return (inv_one, diag_inv_one, inv_two, inv_par, diag_inv_two)


def solution(mesh):
    grid = Mesh(mesh.devices.reshape(4, 4, 4, 2), ("x", "z", "y", "core"))
    row, col = ("x", "z"), ("y", "core")
    return jax.shard_map(
        local,
        mesh=grid,
        in_specs=(
            P(row, col),
            P(col, row),
            P(col, row),
            P(col, None, None),
            P(col, None, None),
            P(col, None, None),
            P(),
            P(),
        ),
        out_specs=(
            P(row, col),
            P(col, None, None),
            P(row, col),
            P(col, None, None),
            P(col, None, None),
        ),
        check_vma=False,
    )
```

```python
import functools

import jax
import jax.numpy as jnp
from jax import lax
from jax.experimental import pallas as pl
from jax.experimental.pallas import tpu as pltpu
from jax.sharding import Mesh, PartitionSpec as P

BLOCK = 256
CHILDREN = 2
HIGH = lax.Precision.HIGH
HIGHEST = lax.Precision.HIGHEST


def fetch(value, axis, shift):
    size = lax.axis_size(axis)
    return lax.ppermute(value, axis, [((i + shift) % size, i) for i in range(size)])


def swap(value):
    return lax.ppermute(value, "core", [(0, 1), (1, 0)])


def split_pairs(step):
    return [(i * 2 + c, (i + (step, -step)[c]) % 4 * 2 + c) for i in range(4) for c in range(2)]


def send(value, axis, step):
    return lax.ppermute(value, (axis, "core"), split_pairs(step))


def after(value, *deps):
    return lax.optimization_barrier((value, *deps))[0] if deps else value


def pick(stack, index):
    return lax.dynamic_index_in_dim(stack, index, axis=0, keepdims=False)


def split(value):
    high = value.astype(jnp.bfloat16)
    return high, (value - high.astype(jnp.float32)).astype(jnp.bfloat16)


def take(refs, to, sems, chosen=None):
    if chosen is None:
        copies = [
            pltpu.make_async_copy(ref, to.at[k], sems.at[k]) for k, ref in enumerate(refs)
        ]
        for copy in copies:
            copy.start()
        return copies
    for k in range(len(refs) // 2):

        @pl.when(chosen == k)
        def _(k=k):
            for p in range(2):
                pltpu.make_async_copy(refs[2 * k + p], to.at[p], sems.at[p]).start()

    return [pltpu.make_async_copy(refs[p], to.at[p], sems.at[p]) for p in range(2)]


def split_strip(strip, strip_high, strip_low, copies):
    deep, chunk = strip.shape[1], 64
    for p in range(2):
        copies[p].wait()

        @pl.loop(0, deep // chunk)
        def _(i, p=p):
            high, low = split(strip[p, pl.ds(i * chunk, chunk), :])
            at = pl.ds(p * deep + i * chunk, chunk)
            strip_high[at, :] = high
            strip_low[at, :] = low


def multiply(out, row_high, row_low, strip_high, strip_low):
    dot = functools.partial(jnp.dot, preferred_element_type=jnp.float32)
    tall = out.shape[0] // 2

    @pl.loop(0, 2)
    def _(r):
        at = pl.ds(pl.multiple_of(r * tall, tall), tall)
        value = dot(row_high[at, :], strip_low[...]) + dot(row_low[at, :], strip_high[...])
        out[at, :] = value + dot(row_high[at, :], strip_high[...])


def first_kernel(places, *refs):
    rows, strips = refs[:4], refs[4:12]
    out_high, out_low, out = refs[12:15]
    row, row_high, row_low, strip, strip_high, strip_low, row_sems, sems = refs[15:]
    strip_copies = take(strips, strip, sems, places[4])
    row_copies = take(rows, row, row_sems)
    split_strip(strip, strip_high, strip_low, strip_copies)
    half, deep = rows[0].shape[1:]
    chunk = 64
    for k, copy in enumerate(row_copies):
        copy.wait()
        first = places[k] * half
        for p in range(2):

            @pl.loop(0, half // chunk)
            def _(i, k=k, p=p, first=first):
                high, low = split(row[k, p, pl.ds(i * chunk, chunk), :])
                at = pl.ds(pl.multiple_of(first + i * chunk, chunk), chunk)
                row_high[at, pl.ds(p * deep, deep)] = high
                row_low[at, pl.ds(p * deep, deep)] = low

    outs = [
        pltpu.make_async_copy(row_high, out_high, row_sems.at[0]),
        pltpu.make_async_copy(row_low, out_low, row_sems.at[1]),
    ]
    for copy in outs:
        copy.start()
    multiply(out, row_high, row_low, strip_high, strip_low)
    for copy in outs:
        copy.wait()


def next_kernel(places, *refs):
    rows, strips = refs[:2], refs[2:10]
    out, row_high, row_low, strip, strip_high, strip_low, row_sems, sems = refs[10:]
    row_copies = [
        pltpu.make_async_copy(ref, to, row_sems.at[p])
        for p, (ref, to) in enumerate(zip(rows, (row_high, row_low)))
    ]
    strip_copies = take(strips, strip, sems, places[0])
    for copy in row_copies:
        copy.start()
    split_strip(strip, strip_high, strip_low, strip_copies)
    for copy in row_copies:
        copy.wait()
    multiply(out, row_high, row_low, strip_high, strip_low)


def product(places, rows, strips, counted=False):
    vmem, hbm = (pl.BlockSpec(memory_space=m) for m in (pltpu.VMEM, pltpu.HBM))
    deep, wide = strips[0].shape
    first = len(rows) == 4
    tall = 4 * rows[0].shape[1] if first else rows[0].shape[0]
    parts = jax.ShapeDtypeStruct((tall, 2 * deep), jnp.bfloat16)
    out = jax.ShapeDtypeStruct((tall, wide), jnp.float32)
    scratch = [pltpu.VMEM((tall, 2 * deep), jnp.bfloat16)] * 2
    scratch += [pltpu.VMEM((2, deep, wide), jnp.float32)]
    scratch += [pltpu.VMEM((2 * deep, wide), jnp.bfloat16)] * 2
    if first:
        scratch = [pltpu.VMEM((4, *rows[0].shape), jnp.float32)] + scratch
    results = pl.pallas_call(
        first_kernel if first else next_kernel,
        out_shape=[parts, parts, out] if first else [out],
        in_specs=[pl.BlockSpec(memory_space=pltpu.SMEM)] + [hbm] * (len(rows) + 8),
        out_specs=[hbm, hbm, vmem] if first else [vmem],
        scratch_shapes=scratch
        + [pltpu.SemaphoreType.DMA((4 if first else 2,)), pltpu.SemaphoreType.DMA((2,))],
        compiler_params=pltpu.CompilerParams(vmem_limit_bytes=56 * 2**20),
        cost_estimate=pl.CostEstimate(
            flops=8 * 10**9 if counted else tall, bytes_accessed=tall, transcendentals=0
        ),
        name="first_product" if first else "next_product",
    )(jnp.stack(places).astype(jnp.int32), *rows, *strips)
    return results if first else results[0]


def dot_in_parts(left, right, contract):
    left, right = split(left), split(right)
    dot = functools.partial(
        lax.dot_general,
        dimension_numbers=((contract[:1], contract[1:]), ((), ())),
        preferred_element_type=jnp.float32,
    )
    return dot(left[0], right[1]) + dot(left[1], right[0]) + dot(left[0], right[0])


def finish_kernel(z, *refs):
    came, (parent, diag_one, diag_two, out_one, out_par, out_two, sums) = refs[:4], refs[4:]
    tall, wide = came[0].shape
    block = parent.shape[1]
    for turn_over, ref in enumerate(came):
        which = z[turn_over]
        at = pl.ds(pl.multiple_of(which % 2 * tall, tall), tall)
        sums[which // 2, at, :] = ref[...]
    part = wide - 2 * block
    first = jnp.concatenate([sums[j, :, pl.ds(0, part)] for j in range(2)], axis=1)
    first = first + diag_one[0]
    out_one[0] = first
    for j in range(2):
        across = sums[j, :, pl.ds(part, block)]
        reach = sums[j, :, pl.ds(part + block, block)]
        par = across - dot_in_parts(first, parent[j], (1, 0))
        out_par[j] = par
        out_two[j] = (
            diag_two[j]
            + reach
            - dot_in_parts(across, parent[j], (0, 0))
            - dot_in_parts(parent[j], par, (0, 0))
        )


def finish(z, came, parent, diag_one, diag_two):
    vmem = pl.BlockSpec(memory_space=pltpu.VMEM)
    tall, wide = came[0].shape
    which = jnp.stack([z ^ turn_over for turn_over in range(4)]).astype(jnp.int32)
    return pl.pallas_call(
        finish_kernel,
        out_shape=[
            jax.ShapeDtypeStruct(v.shape, jnp.float32) for v in (diag_one, parent, diag_two)
        ],
        in_specs=[pl.BlockSpec(memory_space=pltpu.SMEM)] + [vmem] * 7,
        out_specs=[vmem] * 3,
        scratch_shapes=[pltpu.VMEM((2, 2 * tall, wide), jnp.float32)],
        compiler_params=pltpu.CompilerParams(vmem_limit_bytes=24 * 2**20),
        cost_estimate=pl.CostEstimate(flops=10**8, bytes_accessed=10**6, transcendentals=0),
        name="finish",
    )(which, *came, parent, diag_one, diag_two)


def local(
    ancestor_inv, panel_one, panel_two, parent_block, diag_one, diag_two, pattern_one, pattern_two
):
    x, z, y, core = (lax.axis_index(a) for a in ("x", "z", "y", "core"))
    row_index = x * 4 + z
    col_index = y * 2 + core
    panel_rows, w1 = panel_one.shape
    w2 = panel_two.shape[1]
    span = w1 + w2
    half = ancestor_inv.shape[0] // 2
    child_pattern = pattern_two * jnp.repeat(pattern_one, CHILDREN, axis=1)
    with jax.named_scope("gather"):
        halves = ancestor_inv.reshape(2, half, panel_rows)
        given = pick(halves, 1 - core)
        panel_one, panel_two = after(panel_one, given), after(panel_two, given)
        given = swap(given)
    with jax.named_scope("mask"):
        blocks = panel_rows // BLOCK
        mask_one = lax.dynamic_slice(
            pattern_one, (col_index * blocks, row_index // CHILDREN), (blocks, 1)
        )
        mask_two = mask_one * lax.dynamic_slice(
            pattern_two, (col_index * blocks, row_index), (blocks, 1)
        )
        lhs = jnp.concatenate(
            [
                (p.reshape(blocks, BLOCK, -1) * m.astype(jnp.float32)[:, :, None]).reshape(
                    panel_rows, -1
                )
                for p, m in ((panel_one, mask_one), (panel_two, mask_two))
            ],
            axis=1,
        )
    side = jnp.where(core == 0, -1, 1)

    def place(offset):
        offset = offset % 4
        return jnp.where(
            offset == 0, 0, jnp.where(offset == 2, 3, jnp.where(offset == side % 4, 1, 2))
        )

    with jax.named_scope("gather"):
        rows = jnp.stack((pick(halves, core), given))
        lhs = after(lhs, given)
        lhs_other = swap(lhs)
        mine, other = (
            lax.dynamic_index_in_dim(v.reshape(2, 2, half, span), core, axis=1, keepdims=False)
            for v in (lhs, lhs_other)
        )
        source = jnp.concatenate(
            (jnp.where(core == 0, mine, other), jnp.where(core == 0, other, mine)), axis=0
        ).reshape(panel_rows, span)
        source = after(source, rows)
        a_first, a_second = send(rows, "z", 1), send(rows, "z", -1)
        l_first, l_second = send(lhs, "x", 1), send(lhs, "x", -1)
        t_first = send(source, "y", 1)
        t_second = send(after(source, t_first), "y", -1)
        a_first, a_second, l_first, l_second, t_second = lax.optimization_barrier(
            (a_first, a_second, l_first, l_second, t_second)
        )
        a_far, l_far = send(a_first, "z", 1), send(l_first, "x", 1)
        t_far = send(after(t_first, t_second), "y", 1)
        first_other, second_other = swap(l_second), swap(l_first)
        a_far, l_far, first_other, second_other = lax.optimization_barrier(
            (a_far, l_far, first_other, second_other)
        )
        far_other = swap(l_far)

    def spread(values):
        return [
            lax.ppermute(
                value,
                ("z", "core"),
                [
                    ((2 * c + j) * 2 + h, ((2 * j + h) ^ turn_over) * 2 + c)
                    for c in range(2)
                    for j in range(2)
                    for h in range(2)
                ],
            )
            for turn_over, value in enumerate(values)
        ]

    def turn(value, offset, which=0):
        pairs = []
        for i in range(4):
            for c, m in ((0, 1), (1, -1)):
                begin = i + which * m
                end = begin + offset * m
                pairs.append(((begin % 4 * 4 + i) * 2 + c, (end % 4 * 4 + i) * 2 + c))
        return lax.ppermute(value, ("x", "y", "core"), pairs)

    strips = (lhs, lhs_other, l_first, first_other, l_second, second_other, l_far, far_other)
    offsets = (0, side, -side, 2)

    def strip_of(offset):
        return place(y + offset - x)

    with jax.named_scope("product"):
        *parts, far = product(
            [(z + o) % 4 for o in offsets] + [strip_of(2)],
            (rows, a_first, a_second, a_far),
            strips,
        )
        far_came = send(far, "y", 1)
        q_step = turn(after(t_far, l_far), 1)
        q_first = turn(after(t_first, l_far), -1)
        near = product([strip_of(side)], [after(p, far) for p in parts], strips)
        near_came = send(near, "y", -1)
        q_far = turn(after(q_step, near), 1, 1)
        q_second = turn(after(t_second, near), 1)
        last = product([strip_of(-side)], [after(p, near) for p in parts], strips)
        last = last + far_came
        last_came = send(last, "y", 1)
    with jax.named_scope("turned"):
        shift = (x - y) % 4
        q_far = after(q_far, near_came)
        turned = jnp.where(
            shift == 0,
            source,
            jnp.where(
                shift == 2, q_far, jnp.where(shift == side % 4, q_first, q_second)
            ),
        )
        own = turned[:, :w1]
        mate = lax.ppermute(own, "z", [(0, 1), (1, 0), (2, 3), (3, 2)])
        full_one = jnp.concatenate(
            (jnp.where(z % 2 == 0, own, mate), jnp.where(z % 2 == 0, mate, own)), axis=1
        )
    with jax.named_scope("total"):
        rest = product([strip_of(0)], [after(p, last) for p in parts], strips, True)
        rest, near_came, last_came = lax.optimization_barrier((rest, near_came, last_came))
        total = rest + near_came + last_came
    with jax.named_scope("out"):
        pairs_of_rows = total.reshape(2, 2 * half, span)
        kept, came = pick(pairs_of_rows, core), swap(pick(pairs_of_rows, 1 - core))
        kept, came = kept.reshape(2, half, span), came.reshape(2, half, span)
        blocks = jnp.concatenate(
            (jnp.where(core == 0, kept, came), jnp.where(core == 0, came, kept)), axis=1
        )
        pieces = []
        for turn_over in range(2):
            pairs = [
                ((2 * c + j) * 2 + h, (2 * h + (j + turn_over) % 2) * 2 + c)
                for c in range(2)
                for j in range(2)
                for h in range(2)
            ]
            pieces.append(lax.ppermute(pick(blocks, (z + turn_over) % 2), ("z", "core"), pairs))
    with jax.named_scope("quad"):
        quad_one = lax.dot_general(full_one, total, (((0,), (0,)), ((), ())), precision=HIGH)
        quad_two = lax.dot_general(
            turned[:, w1:], total[:, w1:], (((0,), (0,)), ((), ())), precision=HIGH
        )
        quad = jnp.concatenate((quad_one, quad_two), axis=1)
        wide = quad.shape[1]
        quad = quad.reshape(2, BLOCK // 2, wide)
        quad = pick(quad, core) + swap(pick(quad, 1 - core))
        first, second = send(quad, "x", 1), send(quad, "x", -1)
        around = quad + first + second + send(after(first, second, pieces[1]), "x", 1)
        around = after(around, pieces[0])
        came = spread([around] * 4)
    with jax.named_scope("out"):
        joined = [jnp.where(z % 2 == j, pieces[0], pieces[1]) for j in range(2)]
        prod_one = jnp.concatenate([v[:, :w1] for v in joined], axis=1)
        inv_one = -prod_one
        inv_two = jnp.concatenate(
            [
                jnp.dot(prod_one, parent_block[i], precision=HIGH) - joined[i][:, w1:]
                for i in range(2)
            ],
            axis=1,
        )
    with jax.named_scope("diag"):
        diag_inv_one, inv_par, diag_inv_two = finish(z, came, parent_block, diag_one, diag_two)
    return (inv_one, diag_inv_one, inv_two, inv_par, diag_inv_two)


def solution(mesh):
    grid = Mesh(mesh.devices.reshape(4, 4, 4, 2), ("x", "z", "y", "core"))
    row, col = ("x", "z"), ("y", "core")
    return jax.shard_map(
        local,
        mesh=grid,
        in_specs=(
            P(row, col),
            P(col, row),
            P(col, row),
            P(col, None, None),
            P(col, None, None),
            P(col, None, None),
            P(),
            P(),
        ),
        out_specs=(
            P(row, col),
            P(col, None, None),
            P(row, col),
            P(col, None, None),
            P(col, None, None),
        ),
        check_vma=False,
    )
```

```python
import functools

import jax
import jax.numpy as jnp
from jax import lax
from jax.experimental import pallas as pl
from jax.experimental.pallas import tpu as pltpu
from jax.sharding import Mesh, PartitionSpec as P

BLOCK = 256
CHILDREN = 2
HIGH = lax.Precision.HIGH
HIGHEST = lax.Precision.HIGHEST


def fetch(value, axis, shift):
    size = lax.axis_size(axis)
    return lax.ppermute(value, axis, [((i + shift) % size, i) for i in range(size)])


def swap(value):
    return lax.ppermute(value, "core", [(0, 1), (1, 0)])


def split_pairs(step):
    return [(i * 2 + c, (i + (step, -step)[c]) % 4 * 2 + c) for i in range(4) for c in range(2)]


def send(value, axis, step):
    return lax.ppermute(value, (axis, "core"), split_pairs(step))


def after(value, *deps):
    return lax.optimization_barrier((value, *deps))[0] if deps else value


def pick(stack, index):
    return lax.dynamic_index_in_dim(stack, index, axis=0, keepdims=False)


def split(value):
    high = value.astype(jnp.bfloat16)
    return high, (value - high.astype(jnp.float32)).astype(jnp.bfloat16)


def take(refs, to, sems, chosen=None):
    if chosen is None:
        copies = [
            pltpu.make_async_copy(ref, to.at[k], sems.at[k]) for k, ref in enumerate(refs)
        ]
        for copy in copies:
            copy.start()
        return copies
    for k in range(len(refs) // 2):

        @pl.when(chosen == k)
        def _(k=k):
            for p in range(2):
                pltpu.make_async_copy(refs[2 * k + p], to.at[p], sems.at[p]).start()

    return [pltpu.make_async_copy(refs[p], to.at[p], sems.at[p]) for p in range(2)]


def split_strip(strip, strip_high, strip_low, copies):
    deep, chunk = strip.shape[1], 64
    for p in range(2):
        copies[p].wait()

        @pl.loop(0, deep // chunk)
        def _(i, p=p):
            high, low = split(strip[p, pl.ds(i * chunk, chunk), :])
            at = pl.ds(p * deep + i * chunk, chunk)
            strip_high[at, :] = high
            strip_low[at, :] = low


def multiply(out, row_high, row_low, strip_high, strip_low):
    dot = functools.partial(jnp.dot, preferred_element_type=jnp.float32)
    tall = out.shape[0] // 2

    @pl.loop(0, 2)
    def _(r):
        at = pl.ds(pl.multiple_of(r * tall, tall), tall)
        value = dot(row_high[at, :], strip_low[...]) + dot(row_low[at, :], strip_high[...])
        out[at, :] = value + dot(row_high[at, :], strip_high[...])


def first_kernel(places, *refs):
    rows, strips = refs[:4], refs[4:12]
    out_high, out_low, out = refs[12:15]
    row, row_high, row_low, strip, strip_high, strip_low, row_sems, sems = refs[15:]
    strip_copies = take(strips, strip, sems, places[4])
    row_copies = take(rows, row, row_sems)
    split_strip(strip, strip_high, strip_low, strip_copies)
    half, deep = rows[0].shape[1:]
    chunk = 64
    for k, copy in enumerate(row_copies):
        copy.wait()
        first = places[k] * half
        for p in range(2):

            @pl.loop(0, half // chunk)
            def _(i, k=k, p=p, first=first):
                high, low = split(row[k, p, pl.ds(i * chunk, chunk), :])
                at = pl.ds(pl.multiple_of(first + i * chunk, chunk), chunk)
                row_high[at, pl.ds(p * deep, deep)] = high
                row_low[at, pl.ds(p * deep, deep)] = low

    outs = [
        pltpu.make_async_copy(row_high, out_high, row_sems.at[0]),
        pltpu.make_async_copy(row_low, out_low, row_sems.at[1]),
    ]
    for copy in outs:
        copy.start()
    multiply(out, row_high, row_low, strip_high, strip_low)
    for copy in outs:
        copy.wait()


def next_kernel(places, *refs):
    rows, strips = refs[:2], refs[2:10]
    out, row_high, row_low, strip, strip_high, strip_low, row_sems, sems = refs[10:]
    row_copies = [
        pltpu.make_async_copy(ref, to, row_sems.at[p])
        for p, (ref, to) in enumerate(zip(rows, (row_high, row_low)))
    ]
    strip_copies = take(strips, strip, sems, places[0])
    for copy in row_copies:
        copy.start()
    split_strip(strip, strip_high, strip_low, strip_copies)
    for copy in row_copies:
        copy.wait()
    multiply(out, row_high, row_low, strip_high, strip_low)


def product(places, rows, strips, counted=False):
    vmem, hbm = (pl.BlockSpec(memory_space=m) for m in (pltpu.VMEM, pltpu.HBM))
    deep, wide = strips[0].shape
    first = len(rows) == 4
    tall = 4 * rows[0].shape[1] if first else rows[0].shape[0]
    parts = jax.ShapeDtypeStruct((tall, 2 * deep), jnp.bfloat16)
    out = jax.ShapeDtypeStruct((tall, wide), jnp.float32)
    scratch = [pltpu.VMEM((tall, 2 * deep), jnp.bfloat16)] * 2
    scratch += [pltpu.VMEM((2, deep, wide), jnp.float32)]
    scratch += [pltpu.VMEM((2 * deep, wide), jnp.bfloat16)] * 2
    if first:
        scratch = [pltpu.VMEM((4, *rows[0].shape), jnp.float32)] + scratch
    results = pl.pallas_call(
        first_kernel if first else next_kernel,
        out_shape=[parts, parts, out] if first else [out],
        in_specs=[pl.BlockSpec(memory_space=pltpu.SMEM)] + [hbm] * (len(rows) + 8),
        out_specs=[hbm, hbm, vmem] if first else [vmem],
        scratch_shapes=scratch
        + [pltpu.SemaphoreType.DMA((4 if first else 2,)), pltpu.SemaphoreType.DMA((2,))],
        compiler_params=pltpu.CompilerParams(vmem_limit_bytes=56 * 2**20),
        cost_estimate=pl.CostEstimate(
            flops=8 * 10**9 if counted else tall, bytes_accessed=tall, transcendentals=0
        ),
        name="first_product" if first else "next_product",
    )(jnp.stack(places).astype(jnp.int32), *rows, *strips)
    return results if first else results[0]


def dot_in_parts(left, right, contract):
    left, right = split(left), split(right)
    dot = functools.partial(
        lax.dot_general,
        dimension_numbers=((contract[:1], contract[1:]), ((), ())),
        preferred_element_type=jnp.float32,
    )
    return dot(left[0], right[1]) + dot(left[1], right[0]) + dot(left[0], right[0])


def finish_kernel(z, *refs):
    came, (parent, diag_one, diag_two, out_one, out_par, out_two, sums) = refs[:4], refs[4:]
    tall, wide = came[0].shape
    block = parent.shape[1]
    for turn_over, ref in enumerate(came):
        which = z[turn_over]
        at = pl.ds(pl.multiple_of(which % 2 * tall, tall), tall)
        sums[which // 2, at, :] = ref[...]
    part = wide - 2 * block
    first = jnp.concatenate([sums[j, :, pl.ds(0, part)] for j in range(2)], axis=1)
    first = first + diag_one[0]
    out_one[0] = first
    for j in range(2):
        across = sums[j, :, pl.ds(part, block)]
        reach = sums[j, :, pl.ds(part + block, block)]
        par = across - dot_in_parts(first, parent[j], (1, 0))
        out_par[j] = par
        out_two[j] = (
            diag_two[j]
            + reach
            - dot_in_parts(across, parent[j], (0, 0))
            - dot_in_parts(parent[j], par, (0, 0))
        )


def finish(z, came, parent, diag_one, diag_two):
    vmem = pl.BlockSpec(memory_space=pltpu.VMEM)
    tall, wide = came[0].shape
    which = jnp.stack([z ^ turn_over for turn_over in range(4)]).astype(jnp.int32)
    return pl.pallas_call(
        finish_kernel,
        out_shape=[
            jax.ShapeDtypeStruct(v.shape, jnp.float32) for v in (diag_one, parent, diag_two)
        ],
        in_specs=[pl.BlockSpec(memory_space=pltpu.SMEM)] + [vmem] * 7,
        out_specs=[vmem] * 3,
        scratch_shapes=[pltpu.VMEM((2, 2 * tall, wide), jnp.float32)],
        compiler_params=pltpu.CompilerParams(vmem_limit_bytes=24 * 2**20),
        cost_estimate=pl.CostEstimate(flops=10**8, bytes_accessed=10**6, transcendentals=0),
        name="finish",
    )(which, *came, parent, diag_one, diag_two)


def local(
    ancestor_inv, panel_one, panel_two, parent_block, diag_one, diag_two, pattern_one, pattern_two
):
    x, z, y, core = (lax.axis_index(a) for a in ("x", "z", "y", "core"))
    row_index = x * 4 + z
    col_index = y * 2 + core
    panel_rows, w1 = panel_one.shape
    w2 = panel_two.shape[1]
    span = w1 + w2
    half = ancestor_inv.shape[0] // 2
    child_pattern = pattern_two * jnp.repeat(pattern_one, CHILDREN, axis=1)
    with jax.named_scope("gather"):
        halves = ancestor_inv.reshape(2, half, panel_rows)
        given = pick(halves, 1 - core)
        panel_one, panel_two = after(panel_one, given), after(panel_two, given)
        given = swap(given)
    with jax.named_scope("mask"):
        blocks = panel_rows // BLOCK
        mask_one = lax.dynamic_slice(
            pattern_one, (col_index * blocks, row_index // CHILDREN), (blocks, 1)
        )
        mask_two = mask_one * lax.dynamic_slice(
            pattern_two, (col_index * blocks, row_index), (blocks, 1)
        )
        lhs = jnp.concatenate(
            [
                (p.reshape(blocks, BLOCK, -1) * m.astype(jnp.float32)[:, :, None]).reshape(
                    panel_rows, -1
                )
                for p, m in ((panel_one, mask_one), (panel_two, mask_two))
            ],
            axis=1,
        )
    side = jnp.where(core == 0, -1, 1)

    def place(offset):
        offset = offset % 4
        return jnp.where(
            offset == 0, 0, jnp.where(offset == 2, 3, jnp.where(offset == side % 4, 1, 2))
        )

    with jax.named_scope("gather"):
        rows = jnp.stack((pick(halves, core), given))
        lhs = after(lhs, given)
        lhs_other = swap(lhs)
        mine, other = (
            lax.dynamic_index_in_dim(v.reshape(2, 2, half, span), core, axis=1, keepdims=False)
            for v in (lhs, lhs_other)
        )
        source = jnp.concatenate(
            (jnp.where(core == 0, mine, other), jnp.where(core == 0, other, mine)), axis=0
        ).reshape(panel_rows, span)
        source = after(source, rows)
        a_first, a_second = send(rows, "z", 1), send(rows, "z", -1)
        l_first, l_second = send(lhs, "x", 1), send(lhs, "x", -1)
        t_first = send(source, "y", 1)
        t_second = send(after(source, t_first), "y", -1)
        a_first, a_second, l_first, l_second, t_second = lax.optimization_barrier(
            (a_first, a_second, l_first, l_second, t_second)
        )
        a_far, l_far = send(a_first, "z", 1), send(l_first, "x", 1)
        t_far = send(after(t_first, t_second), "y", 1)
        first_other, second_other = swap(l_second), swap(l_first)
        a_far, l_far, t_far, first_other, second_other = lax.optimization_barrier(
            (a_far, l_far, t_far, first_other, second_other)
        )
        far_other = swap(l_far)

    def spread(values):
        return [
            lax.ppermute(
                value,
                ("z", "core"),
                [
                    ((2 * c + j) * 2 + h, ((2 * j + h) ^ turn_over) * 2 + c)
                    for c in range(2)
                    for j in range(2)
                    for h in range(2)
                ],
            )
            for turn_over, value in enumerate(values)
        ]

    def turn(value, offset, which=0):
        pairs = []
        for i in range(4):
            for c, m in ((0, 1), (1, -1)):
                begin = i + which * m
                end = begin + offset * m
                pairs.append(((begin % 4 * 4 + i) * 2 + c, (end % 4 * 4 + i) * 2 + c))
        return lax.ppermute(value, ("x", "y", "core"), pairs)

    strips = (lhs, lhs_other, l_first, first_other, l_second, second_other, l_far, far_other)
    offsets = (0, side, -side, 2)

    def strip_of(offset):
        return place(y + offset - x)

    with jax.named_scope("product"):
        *parts, far = product(
            [(z + o) % 4 for o in offsets] + [strip_of(2)],
            (rows, a_first, a_second, a_far),
            strips,
        )
        far_came = send(far, "y", 1)
        q_step = turn(after(t_far, l_far), 1)
        q_first = turn(after(t_first, l_far), -1)
        near = product([strip_of(side)], [after(p, far) for p in parts], strips)
        near_came = send(near, "y", -1)
        q_far = turn(after(q_step, near), 1, 1)
        q_second = turn(after(t_second, near), 1)
        last = product([strip_of(-side)], [after(p, near) for p in parts], strips)
        last = last + far_came
        last_came = send(last, "y", 1)
    with jax.named_scope("turned"):
        shift = (x - y) % 4
        turned = jnp.where(
            shift == 0,
            source,
            jnp.where(
                shift == 2, q_far, jnp.where(shift == side % 4, q_first, q_second)
            ),
        )
        own = turned[:, :w1]
        mate = lax.ppermute(own, "z", [(0, 1), (1, 0), (2, 3), (3, 2)])
        full_one = jnp.concatenate(
            (jnp.where(z % 2 == 0, own, mate), jnp.where(z % 2 == 0, mate, own)), axis=1
        )
    with jax.named_scope("total"):
        rest = product([strip_of(0)], [after(p, last, turned, near_came) for p in parts], strips, True)
        rest, near_came, last_came = lax.optimization_barrier((rest, near_came, last_came))
        total = rest + near_came + last_came
    with jax.named_scope("out"):
        pairs_of_rows = total.reshape(2, 2 * half, span)
        kept, came = pick(pairs_of_rows, core), swap(pick(pairs_of_rows, 1 - core))
        kept, came = kept.reshape(2, half, span), came.reshape(2, half, span)
        blocks = jnp.concatenate(
            (jnp.where(core == 0, kept, came), jnp.where(core == 0, came, kept)), axis=1
        )
        pieces = []
        for turn_over in range(2):
            pairs = [
                ((2 * c + j) * 2 + h, (2 * h + (j + turn_over) % 2) * 2 + c)
                for c in range(2)
                for j in range(2)
                for h in range(2)
            ]
            pieces.append(lax.ppermute(pick(blocks, (z + turn_over) % 2), ("z", "core"), pairs))
    with jax.named_scope("quad"):
        quad_one = lax.dot_general(full_one, total, (((0,), (0,)), ((), ())), precision=HIGH)
        quad_two = lax.dot_general(
            turned[:, w1:], total[:, w1:], (((0,), (0,)), ((), ())), precision=HIGH
        )
        quad = jnp.concatenate((quad_one, quad_two), axis=1)
        wide = quad.shape[1]
        quad = quad.reshape(2, BLOCK // 2, wide)
        quad = pick(quad, core) + swap(pick(quad, 1 - core))
        first, second = send(quad, "x", 1), send(quad, "x", -1)
        around = quad + first + second + send(after(first, pieces[1]), "x", 1)
        around = after(around, pieces[0])
        came = spread([around] * 4)
    with jax.named_scope("out"):
        joined = [jnp.where(z % 2 == j, pieces[0], pieces[1]) for j in range(2)]
        prod_one = jnp.concatenate([v[:, :w1] for v in joined], axis=1)
        inv_one = -prod_one
        inv_two = jnp.concatenate(
            [
                jnp.dot(prod_one, parent_block[i], precision=HIGH) - joined[i][:, w1:]
                for i in range(2)
            ],
            axis=1,
        )
    with jax.named_scope("diag"):
        diag_inv_one, inv_par, diag_inv_two = finish(z, came, parent_block, diag_one, diag_two)
    return (inv_one, diag_inv_one, inv_two, inv_par, diag_inv_two)


def solution(mesh):
    grid = Mesh(mesh.devices.reshape(4, 4, 4, 2), ("x", "z", "y", "core"))
    row, col = ("x", "z"), ("y", "core")
    return jax.shard_map(
        local,
        mesh=grid,
        in_specs=(
            P(row, col),
            P(col, row),
            P(col, row),
            P(col, None, None),
            P(col, None, None),
            P(col, None, None),
            P(),
            P(),
        ),
        out_specs=(
            P(row, col),
            P(col, None, None),
            P(row, col),
            P(col, None, None),
            P(col, None, None),
        ),
        check_vma=False,
    )
```

```python
import functools

import jax
import jax.numpy as jnp
from jax import lax
from jax.experimental import pallas as pl
from jax.experimental.pallas import tpu as pltpu
from jax.sharding import Mesh, PartitionSpec as P

BLOCK = 256
CHILDREN = 2
HIGH = lax.Precision.HIGH
HIGHEST = lax.Precision.HIGHEST


def fetch(value, axis, shift):
    size = lax.axis_size(axis)
    return lax.ppermute(value, axis, [((i + shift) % size, i) for i in range(size)])


def swap(value):
    return lax.ppermute(value, "core", [(0, 1), (1, 0)])


def split_pairs(step):
    return [(i * 2 + c, (i + (step, -step)[c]) % 4 * 2 + c) for i in range(4) for c in range(2)]


def send(value, axis, step):
    return lax.ppermute(value, (axis, "core"), split_pairs(step))


def after(value, *deps):
    return lax.optimization_barrier((value, *deps))[0] if deps else value


def pick(stack, index):
    return lax.dynamic_index_in_dim(stack, index, axis=0, keepdims=False)


def split(value):
    high = value.astype(jnp.bfloat16)
    return high, (value - high.astype(jnp.float32)).astype(jnp.bfloat16)


def take(refs, to, sems, chosen=None):
    if chosen is None:
        copies = [
            pltpu.make_async_copy(ref, to.at[k], sems.at[k]) for k, ref in enumerate(refs)
        ]
        for copy in copies:
            copy.start()
        return copies
    for k in range(len(refs) // 2):

        @pl.when(chosen == k)
        def _(k=k):
            for p in range(2):
                pltpu.make_async_copy(refs[2 * k + p], to.at[p], sems.at[p]).start()

    return [pltpu.make_async_copy(refs[p], to.at[p], sems.at[p]) for p in range(2)]


def split_strip(strip, strip_high, strip_low, copies):
    deep, chunk = strip.shape[1], 64
    for p in range(2):
        copies[p].wait()

        @pl.loop(0, deep // chunk)
        def _(i, p=p):
            high, low = split(strip[p, pl.ds(i * chunk, chunk), :])
            at = pl.ds(p * deep + i * chunk, chunk)
            strip_high[at, :] = high
            strip_low[at, :] = low


def multiply(out, row_high, row_low, strip_high, strip_low):
    dot = functools.partial(jnp.dot, preferred_element_type=jnp.float32)
    tall = out.shape[0] // 2

    @pl.loop(0, 2)
    def _(r):
        at = pl.ds(pl.multiple_of(r * tall, tall), tall)
        value = dot(row_high[at, :], strip_low[...]) + dot(row_low[at, :], strip_high[...])
        out[at, :] = value + dot(row_high[at, :], strip_high[...])


def first_kernel(places, *refs):
    rows, strips = refs[:4], refs[4:12]
    out_high, out_low, out = refs[12:15]
    row, row_high, row_low, strip, strip_high, strip_low, row_sems, sems = refs[15:]
    strip_copies = take(strips, strip, sems, places[4])
    row_copies = take(rows, row, row_sems)
    split_strip(strip, strip_high, strip_low, strip_copies)
    half, deep = rows[0].shape[1:]
    chunk = 64
    for k, copy in enumerate(row_copies):
        copy.wait()
        first = places[k] * half
        for p in range(2):

            @pl.loop(0, half // chunk)
            def _(i, k=k, p=p, first=first):
                high, low = split(row[k, p, pl.ds(i * chunk, chunk), :])
                at = pl.ds(pl.multiple_of(first + i * chunk, chunk), chunk)
                row_high[at, pl.ds(p * deep, deep)] = high
                row_low[at, pl.ds(p * deep, deep)] = low

    outs = [
        pltpu.make_async_copy(row_high, out_high, row_sems.at[0]),
        pltpu.make_async_copy(row_low, out_low, row_sems.at[1]),
    ]
    for copy in outs:
        copy.start()
    multiply(out, row_high, row_low, strip_high, strip_low)
    for copy in outs:
        copy.wait()


def next_kernel(places, *refs):
    rows, strips = refs[:2], refs[2:10]
    out, row_high, row_low, strip, strip_high, strip_low, row_sems, sems = refs[10:]
    row_copies = [
        pltpu.make_async_copy(ref, to, row_sems.at[p])
        for p, (ref, to) in enumerate(zip(rows, (row_high, row_low)))
    ]
    strip_copies = take(strips, strip, sems, places[0])
    for copy in row_copies:
        copy.start()
    split_strip(strip, strip_high, strip_low, strip_copies)
    for copy in row_copies:
        copy.wait()
    multiply(out, row_high, row_low, strip_high, strip_low)


def product(places, rows, strips, counted=False):
    vmem, hbm = (pl.BlockSpec(memory_space=m) for m in (pltpu.VMEM, pltpu.HBM))
    deep, wide = strips[0].shape
    first = len(rows) == 4
    tall = 4 * rows[0].shape[1] if first else rows[0].shape[0]
    parts = jax.ShapeDtypeStruct((tall, 2 * deep), jnp.bfloat16)
    out = jax.ShapeDtypeStruct((tall, wide), jnp.float32)
    scratch = [pltpu.VMEM((tall, 2 * deep), jnp.bfloat16)] * 2
    scratch += [pltpu.VMEM((2, deep, wide), jnp.float32)]
    scratch += [pltpu.VMEM((2 * deep, wide), jnp.bfloat16)] * 2
    if first:
        scratch = [pltpu.VMEM((4, *rows[0].shape), jnp.float32)] + scratch
    results = pl.pallas_call(
        first_kernel if first else next_kernel,
        out_shape=[parts, parts, out] if first else [out],
        in_specs=[pl.BlockSpec(memory_space=pltpu.SMEM)] + [hbm] * (len(rows) + 8),
        out_specs=[hbm, hbm, vmem] if first else [vmem],
        scratch_shapes=scratch
        + [pltpu.SemaphoreType.DMA((4 if first else 2,)), pltpu.SemaphoreType.DMA((2,))],
        compiler_params=pltpu.CompilerParams(vmem_limit_bytes=56 * 2**20),
        cost_estimate=pl.CostEstimate(
            flops=8 * 10**9 if counted else tall, bytes_accessed=tall, transcendentals=0
        ),
        name="first_product" if first else "next_product",
    )(jnp.stack(places).astype(jnp.int32), *rows, *strips)
    return results if first else results[0]


def dot_in_parts(left, right, contract):
    left, right = split(left), split(right)
    dot = functools.partial(
        lax.dot_general,
        dimension_numbers=((contract[:1], contract[1:]), ((), ())),
        preferred_element_type=jnp.float32,
    )
    return dot(left[0], right[1]) + dot(left[1], right[0]) + dot(left[0], right[0])


def finish_kernel(z, *refs):
    came, (parent, diag_one, diag_two, out_one, out_par, out_two, sums) = refs[:4], refs[4:]
    tall, wide = came[0].shape
    block = parent.shape[1]
    for turn_over, ref in enumerate(came):
        which = z[turn_over]
        at = pl.ds(pl.multiple_of(which % 2 * tall, tall), tall)
        sums[which // 2, at, :] = ref[...]
    part = wide - 2 * block
    first = jnp.concatenate([sums[j, :, pl.ds(0, part)] for j in range(2)], axis=1)
    first = first + diag_one[0]
    out_one[0] = first
    for j in range(2):
        across = sums[j, :, pl.ds(part, block)]
        reach = sums[j, :, pl.ds(part + block, block)]
        par = across - dot_in_parts(first, parent[j], (1, 0))
        out_par[j] = par
        out_two[j] = (
            diag_two[j]
            + reach
            - dot_in_parts(across, parent[j], (0, 0))
            - dot_in_parts(parent[j], par, (0, 0))
        )


def finish(z, came, parent, diag_one, diag_two):
    vmem = pl.BlockSpec(memory_space=pltpu.VMEM)
    tall, wide = came[0].shape
    which = jnp.stack([z ^ turn_over for turn_over in range(4)]).astype(jnp.int32)
    return pl.pallas_call(
        finish_kernel,
        out_shape=[
            jax.ShapeDtypeStruct(v.shape, jnp.float32) for v in (diag_one, parent, diag_two)
        ],
        in_specs=[pl.BlockSpec(memory_space=pltpu.SMEM)] + [vmem] * 7,
        out_specs=[vmem] * 3,
        scratch_shapes=[pltpu.VMEM((2, 2 * tall, wide), jnp.float32)],
        compiler_params=pltpu.CompilerParams(vmem_limit_bytes=24 * 2**20),
        cost_estimate=pl.CostEstimate(flops=10**8, bytes_accessed=10**6, transcendentals=0),
        name="finish",
    )(which, *came, parent, diag_one, diag_two)


def local(
    ancestor_inv, panel_one, panel_two, parent_block, diag_one, diag_two, pattern_one, pattern_two
):
    x, z, y, core = (lax.axis_index(a) for a in ("x", "z", "y", "core"))
    row_index = x * 4 + z
    col_index = y * 2 + core
    panel_rows, w1 = panel_one.shape
    w2 = panel_two.shape[1]
    span = w1 + w2
    half = ancestor_inv.shape[0] // 2
    child_pattern = pattern_two * jnp.repeat(pattern_one, CHILDREN, axis=1)
    with jax.named_scope("gather"):
        halves = ancestor_inv.reshape(2, half, panel_rows)
        given = pick(halves, 1 - core)
        panel_one, panel_two = after(panel_one, given), after(panel_two, given)
        given = swap(given)
    with jax.named_scope("mask"):
        blocks = panel_rows // BLOCK
        mask_one = lax.dynamic_slice(
            pattern_one, (col_index * blocks, row_index // CHILDREN), (blocks, 1)
        )
        mask_two = mask_one * lax.dynamic_slice(
            pattern_two, (col_index * blocks, row_index), (blocks, 1)
        )
        lhs = jnp.concatenate(
            [
                (p.reshape(blocks, BLOCK, -1) * m.astype(jnp.float32)[:, :, None]).reshape(
                    panel_rows, -1
                )
                for p, m in ((panel_one, mask_one), (panel_two, mask_two))
            ],
            axis=1,
        )
    side = jnp.where(core == 0, -1, 1)

    def place(offset):
        offset = offset % 4
        return jnp.where(
            offset == 0, 0, jnp.where(offset == 2, 3, jnp.where(offset == side % 4, 1, 2))
        )

    with jax.named_scope("gather"):
        rows = jnp.stack((pick(halves, core), given))
        lhs = after(lhs, given)
        lhs_other = swap(lhs)
        mine, other = (
            lax.dynamic_index_in_dim(v.reshape(2, 2, half, span), core, axis=1, keepdims=False)
            for v in (lhs, lhs_other)
        )
        source = jnp.concatenate(
            (jnp.where(core == 0, mine, other), jnp.where(core == 0, other, mine)), axis=0
        ).reshape(panel_rows, span)
        source = after(source, rows)
        a_first, a_second = send(rows, "z", 1), send(rows, "z", -1)
        l_first, l_second = send(lhs, "x", 1), send(lhs, "x", -1)
        t_first = send(source, "y", 1)
        t_second = send(after(source, t_first), "y", -1)
        a_first, a_second, l_first, l_second, t_second = lax.optimization_barrier(
            (a_first, a_second, l_first, l_second, t_second)
        )
        a_far, l_far = send(a_first, "z", 1), send(l_first, "x", 1)
        t_far = send(after(t_first, t_second), "y", 1)
        first_other, second_other = swap(l_second), swap(l_first)
        a_far, l_far, first_other, second_other = lax.optimization_barrier(
            (a_far, l_far, first_other, second_other)
        )
        far_other = swap(l_far)

    def spread(values):
        return [
            lax.ppermute(
                value,
                ("z", "core"),
                [
                    ((2 * c + j) * 2 + h, ((2 * j + h) ^ turn_over) * 2 + c)
                    for c in range(2)
                    for j in range(2)
                    for h in range(2)
                ],
            )
            for turn_over, value in enumerate(values)
        ]

    def turn(value, offset, which=0):
        pairs = []
        for i in range(4):
            for c, m in ((0, 1), (1, -1)):
                begin = i + which * m
                end = begin + offset * m
                pairs.append(((begin % 4 * 4 + i) * 2 + c, (end % 4 * 4 + i) * 2 + c))
        return lax.ppermute(value, ("x", "y", "core"), pairs)

    strips = (lhs, lhs_other, l_first, first_other, l_second, second_other, l_far, far_other)
    offsets = (0, side, -side, 2)

    def strip_of(offset):
        return place(y + offset - x)

    with jax.named_scope("product"):
        *parts, far = product(
            [(z + o) % 4 for o in offsets] + [strip_of(2)],
            (rows, a_first, a_second, a_far),
            strips,
        )
        far_came = send(far, "y", 1)
        q_step = turn(after(t_far, l_far), 1)
        q_first = turn(after(t_first, l_far), -1)
        near = product([strip_of(side)], [after(p, far) for p in parts], strips)
        near_came = send(near, "y", -1)
        q_far = turn(after(q_step, near), 1, 1)
        q_second = turn(after(t_second, near), 1)
        last = product([strip_of(-side)], [after(p, near) for p in parts], strips)
        last = last + far_came
        last_came = send(last, "y", 1)
    with jax.named_scope("turned"):
        shift = (x - y) % 4
        turned = jnp.where(
            shift == 0,
            source,
            jnp.where(
                shift == 2, q_far, jnp.where(shift == side % 4, q_first, q_second)
            ),
        )
        own = turned[:, :w1]
        mate = lax.ppermute(own, "z", [(0, 1), (1, 0), (2, 3), (3, 2)])
        full_one = jnp.concatenate(
            (jnp.where(z % 2 == 0, own, mate), jnp.where(z % 2 == 0, mate, own)), axis=1
        )
    with jax.named_scope("total"):
        rest = product([strip_of(0)], [after(p, last, turned, near_came) for p in parts], strips, True)
        rest, near_came, last_came = lax.optimization_barrier((rest, near_came, last_came))
        total = rest + near_came + last_came
    with jax.named_scope("out"):
        pairs_of_rows = total.reshape(2, 2 * half, span)
        kept, came = pick(pairs_of_rows, core), swap(pick(pairs_of_rows, 1 - core))
        kept, came = kept.reshape(2, half, span), came.reshape(2, half, span)
        blocks = jnp.concatenate(
            (jnp.where(core == 0, kept, came), jnp.where(core == 0, came, kept)), axis=1
        )
        pieces = []
        for turn_over in range(2):
            pairs = [
                ((2 * c + j) * 2 + h, (2 * h + (j + turn_over) % 2) * 2 + c)
                for c in range(2)
                for j in range(2)
                for h in range(2)
            ]
            pieces.append(lax.ppermute(pick(blocks, (z + turn_over) % 2), ("z", "core"), pairs))
    with jax.named_scope("quad"):
        quad_one = lax.dot_general(full_one, total, (((0,), (0,)), ((), ())), precision=HIGH)
        quad_two = lax.dot_general(
            turned[:, w1:], total[:, w1:], (((0,), (0,)), ((), ())), precision=HIGH
        )
        quad = jnp.concatenate((quad_one, quad_two), axis=1)
        wide = quad.shape[1]
        quad = quad.reshape(2, BLOCK // 2, wide)
        quad = pick(quad, core) + swap(pick(quad, 1 - core))
        first, second = send(quad, "x", 1), send(quad, "x", -1)
        around = quad + first + second + send(after(first, pieces[1]), "x", 1)
        around = after(around, pieces[0])
        came = spread([around] * 4)
    with jax.named_scope("out"):
        joined = [jnp.where(z % 2 == j, pieces[0], pieces[1]) for j in range(2)]
        prod_one = jnp.concatenate([v[:, :w1] for v in joined], axis=1)
        inv_one = -prod_one
        inv_two = jnp.concatenate(
            [
                jnp.dot(prod_one, parent_block[i], precision=HIGH) - joined[i][:, w1:]
                for i in range(2)
            ],
            axis=1,
        )
    with jax.named_scope("diag"):
        diag_inv_one, inv_par, diag_inv_two = finish(z, came, parent_block, diag_one, diag_two)
    return (inv_one, diag_inv_one, inv_two, inv_par, diag_inv_two)


def solution(mesh):
    grid = Mesh(mesh.devices.reshape(4, 4, 4, 2), ("x", "z", "y", "core"))
    row, col = ("x", "z"), ("y", "core")
    return jax.shard_map(
        local,
        mesh=grid,
        in_specs=(
            P(row, col),
            P(col, row),
            P(col, row),
            P(col, None, None),
            P(col, None, None),
            P(col, None, None),
            P(),
            P(),
        ),
        out_specs=(
            P(row, col),
            P(col, None, None),
            P(row, col),
            P(col, None, None),
            P(col, None, None),
        ),
        check_vma=False,
    )
```
